128 devices in a mesh: gx: 16 (over x, y), gy: 8 (over z, core).
Axes of the slice: x: 4, y: 4, z: 4, core: 2. Of those that a mesh axis runs over, the one named last changes fastest.
Arguments:
- tokens: bfloat16 [16384, 2048], P(('gx', 'gy')), may hold values from -6 to 6
- out_grad: bfloat16 [16384, 2048], P(('gx', 'gy')), may hold values from -1.5 to 1.5
- expert_ids: int32 [16384, 8], P(('gx', 'gy')), may hold values from 0 to 127, all different within a row; in each aligned block of 128 rows (0 to 127, 128 to 255, ...) at most 9 rows name the same one
- gate_weights: bfloat16 [16384, 8], P(('gx', 'gy')), may hold values from 0.029907227 to 0.29882812
- w_gate: bfloat16 [128, 2048, 768], P(('gx', 'gy')), may hold values from -0.125 to 0.125
- w_up: bfloat16 [128, 2048, 768], P(('gx', 'gy')), may hold values from -0.125 to 0.125
- w_down: bfloat16 [128, 768, 2048], P(('gx', 'gy')), may hold values from -0.21875 to 0.21875
Outputs:
- token_grad: bfloat16 [16384, 2048], P(('gx', 'gy'))
- gate_grad: bfloat16 [16384, 8], P(('gx', 'gy'))
- grad_w_gate: bfloat16 [128, 2048, 768], P(('gx', 'gy'))
- grad_w_up: bfloat16 [128, 2048, 768], P(('gx', 'gy'))
- grad_w_down: bfloat16 [128, 768, 2048], P(('gx', 'gy'))
The draws below stay inside these ranges and needn't reach their ends.
Inputs may be any that keep to these rules, and one draw needn't show every extreme that they name: `expert_ids`: each token names 8 different experts; among the 128 tokens of one device (an aligned block of rows) no expert is named more than 9 times, a bound that some block reaches.
All inputs are finite; a program needn't handle non-finite values.
Results may differ from the reference program's by a relative error of at most 0.011.
Values may be sent and summed in bfloat16 or wider, within the bound.
A program may use at most 128 MiB of HBM per device.

```python
import math
import jax
import jax.numpy as jnp
import numpy as np
from jax import lax

D = 2048
FF = 768
TOP = 8
TOK_DEV = 128
EXPERTS = 128
TOKENS = 16384
CAP = 9
N_GX = 16
N_GY = 8


def level_of(key, shape, shards, least, top_value):
    loudness, own = 1.0, jax.random.fold_in(key, 6)
    for dim, parts in shards:
        steps = jnp.exp(jax.random.uniform(jax.random.fold_in(own, dim), (parts,), jnp.float32, least / len(shards), top_value / len(shards)))
        loudness = loudness * jnp.repeat(steps, shape[dim] // parts).reshape([-1 if axis == dim else 1 for axis in range(len(shape))])
    return loudness


def shared_out(rng, own, number, rows, amount, top, bound, skew):
    order = jax.random.permutation(rng, amount)
    heavy_load, usual = shares(amount, rows * top, bound, skew, True), shares(amount, rows * top, bound, skew, False)
    places = jnp.arange(amount)

    def named(sizes, rotation):
        used = int((sizes > 0).sum())
        fixed = max(1, used // 4)
        moved = fixed + (places - fixed + rotation * (used - fixed)) % max(1, amount - fixed)
        return jnp.zeros((amount,), jnp.int32).at[order[jnp.where(places < fixed, places, moved)]].set(jnp.asarray(sizes, jnp.int32))

    sizes = jnp.where(number % 4 == 0, named(heavy_load, number // 4), named(usual, number - number // 4 - 1))
    mixed = jax.random.permutation(jax.random.fold_in(own, 3), amount)
    giver, sink = mixed[0:amount // 2 * 2:2], mixed[1:amount // 2 * 2:2]
    slack = jnp.minimum(sizes[giver] - 1, bound - sizes[sink]) // 2
    slack = jnp.where((giver == order[0]) | (sink == order[0]) | (sizes[sink] == 0), 0, jnp.maximum(slack, 0))
    moved = jax.random.randint(jax.random.fold_in(own, 4), (amount // 2,), 0, 1 << 20) % (slack + 1)
    sizes = sizes.at[giver].add(-moved).at[sink].add(moved)
    labels = jnp.searchsorted(jnp.cumsum(sizes), jnp.arange(rows * top), side="right").astype(jnp.int32)
    grid = labels.reshape(top, rows).T
    grid = grid[jax.random.permutation(jax.random.fold_in(own, 1), rows)]
    rotation = jax.random.randint(jax.random.fold_in(own, 2), (rows, 1), 0, top)
    return jnp.take_along_axis(grid, (jnp.arange(top)[None, :] + rotation) % top, axis=1)


def shares(amount, total, limit, slope, full):
    portions = [(1 << 20) // math.isqrt(standing ** slope) + 1 for standing in range(1, amount + 1)]
    largest = limit if full else min(limit, max(-(-total // amount), total * portions[0] // sum(portions)))
    least = 1 if total - largest >= amount - 1 else 0
    counts, spare = [largest] + [least] * (amount - 1), total - largest - least * (amount - 1)
    while spare > 0:
        free = [i for i in range(1, amount) if counts[i] < largest] or [i for i in range(1, amount) if counts[i] < limit]
        mass, left = sum([portions[i] for i in free]), spare
        for i in free:
            addition = min(limit - counts[i], max(1, left * portions[i] // mass), spare)
            counts[i] = counts[i] + addition
            spare = spare - addition
    return np.array(counts)


def gaussian(stream_key, extent, scale, bound, split=(), kind=jnp.bfloat16):
    entries = scale * jax.random.normal(stream_key, extent, jnp.float32)
    if split:
        entries = entries * level_of(stream_key, extent, split, -0.22, 0.18)
    return jnp.clip(entries, -bound, bound).astype(kind)


def setup_inputs(seed: int = 0) -> dict:
    keys = jax.random.split(jax.random.key(seed), 8)
    tokens = gaussian(keys[0], (TOKENS, D), 1.0, 6.0, ((0, 128),))
    out_grad = gaussian(keys[1], (TOKENS, D), 0.25, 1.5, ((0, 128),))
    expert_ids_keys = jax.random.split(jax.random.fold_in(keys[2], 1), TOKENS // TOK_DEV)
    expert_ids_turns = jax.random.permutation(jax.random.fold_in(keys[2], 3), TOKENS // TOK_DEV)
    expert_ids = jax.vmap(lambda own, number: shared_out(jax.random.fold_in(keys[2], 2), own, number, TOK_DEV, EXPERTS, TOP, CAP, 2))(expert_ids_keys, expert_ids_turns).reshape((TOKENS, TOP))
    gate_weights = jnp.clip(jnp.exp(math.log(0.29882812) - 2.30176843 * jax.random.uniform(keys[3], (TOKENS, TOP), jnp.float32) ** level_of(keys[3], (TOKENS, TOP), ((0, 128),), -0.2, 0.2)), 0.029907227, 0.29882812).astype(jnp.bfloat16)
    w_gate = gaussian(keys[4], (EXPERTS, D, FF), D ** -0.5, 0.125, ((0, 128),))
    w_up = gaussian(keys[5], (EXPERTS, D, FF), D ** -0.5, 0.125, ((0, 128),))
    w_down = gaussian(keys[6], (EXPERTS, FF, D), FF ** -0.5, 0.21875, ((0, 128),))
    return dict(tokens=tokens, out_grad=out_grad, expert_ids=expert_ids, gate_weights=gate_weights, w_gate=w_gate, w_up=w_up, w_down=w_down)


def expert_step(carry, inputs):
    token_acc, gate_acc, tokens, out_grad, gate_flat = carry
    pair_row, wg, wu, wd = inputs
    valid = pair_row >= 0
    pair_safe = jnp.maximum(pair_row, 0)
    token_row = pair_safe // TOP
    x_rows = jnp.where(valid[:, None], tokens[token_row], jnp.zeros((), jnp.bfloat16))
    dy_rows = jnp.where(valid[:, None], out_grad[token_row], jnp.zeros((), jnp.bfloat16))
    gate_col = jnp.where(valid, gate_flat[pair_safe].astype(jnp.float32), jnp.float32(0.0))[:, None]
    pre_gate = jnp.dot(x_rows, wg, preferred_element_type=jnp.float32)
    pre_up = jnp.dot(x_rows, wu, preferred_element_type=jnp.float32)
    sigma = jax.nn.sigmoid(pre_gate)
    silu_val = pre_gate * sigma
    act = (silu_val * pre_up).astype(jnp.bfloat16)
    back = jnp.dot(dy_rows, wd.T, preferred_element_type=jnp.float32)
    pair_gate = jnp.sum(back * act.astype(jnp.float32), axis=1).astype(jnp.bfloat16)
    scaled_back = gate_col * back
    grad_up = (scaled_back * silu_val).astype(jnp.bfloat16)
    grad_pre = (scaled_back * pre_up * sigma * (1.0 + pre_gate * (1.0 - sigma))).astype(jnp.bfloat16)
    scaled_grad = (gate_col * dy_rows.astype(jnp.float32)).astype(jnp.bfloat16)
    contract = (((0,), (0,)), ((), ()))
    gw_down = lax.dot_general(act, scaled_grad, contract, preferred_element_type=jnp.float32).astype(jnp.bfloat16)
    gw_gate = lax.dot_general(x_rows, grad_pre, contract, preferred_element_type=jnp.float32).astype(jnp.bfloat16)
    gw_up = lax.dot_general(x_rows, grad_up, contract, preferred_element_type=jnp.float32).astype(jnp.bfloat16)
    pair_input = (jnp.dot(grad_pre, wg.T, preferred_element_type=jnp.float32)
                  + jnp.dot(grad_up, wu.T, preferred_element_type=jnp.float32)).astype(jnp.bfloat16)
    token_acc = token_acc.at[token_row].add(jnp.where(valid[:, None], pair_input.astype(jnp.float32), jnp.float32(0.0)))
    gate_acc = gate_acc.at[pair_safe].add(jnp.where(valid, pair_gate.astype(jnp.float32), jnp.float32(0.0)))
    return (token_acc, gate_acc, tokens, out_grad, gate_flat), (gw_gate, gw_up, gw_down)


def reference(tokens, out_grad, expert_ids, gate_weights, w_gate, w_up, w_down):
    blocks = N_GX * N_GY
    flat_ids = expert_ids.reshape(blocks, TOK_DEV * TOP)
    onehot = (flat_ids[:, :, None] == jnp.arange(EXPERTS, dtype=jnp.int32)[None, None, :]).astype(jnp.int32)
    ranks = jnp.sum(jnp.cumsum(onehot, axis=1) * onehot, axis=2) - 1
    slot_ids = flat_ids * (blocks * CAP) + jnp.arange(blocks, dtype=jnp.int32)[:, None] * CAP + ranks
    table = jnp.full((EXPERTS * blocks * CAP,), -1, jnp.int32)
    table = table.at[slot_ids.reshape(-1)].set(jnp.arange(TOKENS * TOP, dtype=jnp.int32))
    table = table.reshape(EXPERTS, blocks * CAP)
    token_acc = jnp.zeros((TOKENS, D), jnp.float32)
    gate_acc = jnp.zeros((TOKENS * TOP,), jnp.float32)
    carry = (token_acc, gate_acc, tokens, out_grad, gate_weights.reshape(-1))
    carry, grads = lax.scan(expert_step, carry, (table, w_gate, w_up, w_down))
    token_grad = carry[0].astype(jnp.bfloat16)
    gate_grad = carry[1].reshape(TOKENS, TOP).astype(jnp.bfloat16)
    return (token_grad, gate_grad, grads[0], grads[1], grads[2])
```

```python
import jax
import jax.numpy as jnp
from jax import lax
from jax.sharding import PartitionSpec as P

BF = jnp.bfloat16
F32 = jnp.float32


def expert_backward(x_rows, sdy_rows, wg, wu, wd):
    right = (((1,), (1,)), ((), ()))
    contract = (((0,), (0,)), ((), ()))
    pre_gate = jnp.dot(x_rows, wg, preferred_element_type=F32)
    pre_up = jnp.dot(x_rows, wu, preferred_element_type=F32)
    sigma = jax.nn.sigmoid(pre_gate)
    silu_val = pre_gate * sigma
    act = (silu_val * pre_up).astype(BF)
    scaled_back = lax.dot_general(sdy_rows, wd, right, preferred_element_type=F32)
    scaled_gate = jnp.sum(scaled_back * act.astype(F32), axis=1)
    grad_up = (scaled_back * silu_val).astype(BF)
    grad_pre = (scaled_back * pre_up * sigma * (1.0 + pre_gate * (1.0 - sigma))).astype(BF)
    gw_down = lax.dot_general(act, sdy_rows, contract, preferred_element_type=F32).astype(BF)
    gw_gate = lax.dot_general(x_rows, grad_pre, contract, preferred_element_type=F32).astype(BF)
    gw_up = lax.dot_general(x_rows, grad_up, contract, preferred_element_type=F32).astype(BF)
    pair_input = (
        lax.dot_general(grad_pre, wg, right, preferred_element_type=F32)
        + lax.dot_general(grad_up, wu, right, preferred_element_type=F32)
    ).astype(BF)
    return pair_input, scaled_gate, gw_gate, gw_up, gw_down


def on_device(tokens, out_grad, expert_ids, gate_weights, w_gate, w_up, w_down):
    peers = lax.axis_size("gx") * lax.axis_size("gy")
    tok, top = expert_ids.shape
    width = tokens.shape[1]
    cap = tok * top // peers + 1
    tiles = width // 128
    named = (expert_ids[:, :, None] == jnp.arange(peers, dtype=jnp.int32)).astype(F32)
    member = jnp.sum(named, axis=1)
    gate_of = jnp.sum(named * gate_weights.astype(F32)[:, :, None], axis=1)
    earlier = (jnp.arange(tok)[:, None] > jnp.arange(tok)[None, :]).astype(BF)
    rank = jnp.dot(earlier, member.astype(BF), preferred_element_type=F32)
    rank_t, member_t, gate_t = rank.T, member.T, gate_of.T
    slot = jnp.arange(cap, dtype=F32)[None, :, None]
    pick = (rank_t[:, None, :] == slot) & (member_t[:, None, :] > 0)
    pick = pick.astype(F32)
    gate_slot = jnp.sum(pick * gate_t[:, None, :], axis=2)
    pick = pick.reshape(peers * cap, tok).astype(BF)
    x_send = jnp.dot(pick, tokens, preferred_element_type=F32).astype(BF)
    dy_send = jnp.dot(pick, out_grad, preferred_element_type=F32)
    dy_send = (dy_send * gate_slot.reshape(peers * cap, 1)).astype(BF)
    send = jnp.stack(
        [x_send.reshape(peers, cap, tiles, 128), dy_send.reshape(peers, cap, tiles, 128)], axis=1
    )
    recv = lax.all_to_all(send, ("gx", "gy"), split_axis=0, concat_axis=0, tiled=True)
    pair_input, scaled_gate, gw_gate, gw_up, gw_down = expert_backward(
        recv[:, 0].reshape(peers * cap, width),
        recv[:, 1].reshape(peers * cap, width),
        w_gate[0],
        w_up[0],
        w_down[0],
    )
    input_back = lax.all_to_all(
        pair_input.reshape(peers, cap, tiles, 128), ("gx", "gy"), split_axis=0, concat_axis=0, tiled=True
    )
    gate_back = lax.all_to_all(
        scaled_gate.reshape(peers, cap), ("gx", "gy"), split_axis=0, concat_axis=0, tiled=True
    )
    token_grad = lax.dot_general(
        pick,
        input_back.reshape(peers * cap, width),
        (((0,), (0,)), ((), ())),
        preferred_element_type=F32,
    ).astype(BF)
    pick3 = pick.reshape(peers, cap, tok).astype(F32)
    gate_pair = jnp.sum(pick3 * gate_back[:, :, None], axis=1).T
    gate_grad = jnp.sum(named * gate_pair[:, None, :], axis=2) / gate_weights.astype(F32)
    return (token_grad, gate_grad.astype(BF), gw_gate[None], gw_up[None], gw_down[None])


def solution(mesh):
    both = ("gx", "gy")
    return jax.shard_map(
        on_device,
        mesh=mesh,
        in_specs=(P(both, None),) * 4 + (P(both, None, None),) * 3,
        out_specs=(P(both, None),) * 2 + (P(both, None, None),) * 3,
        check_vma=False,
    )
```

```python
import functools

import jax
import jax.numpy as jnp
from jax import lax
from jax.experimental import pallas as pl
from jax.experimental.pallas import tpu as pltpu
from jax.sharding import PartitionSpec as P

BF = jnp.bfloat16
F32 = jnp.float32
PEERS = 128
CAP = 9
GROUPS = 4
PER = PEERS // GROUPS
ROWS = PER * CAP
TILES = 16
MESH = pl.DeviceIdType.MESH
RIGHT = (((1,), (1,)), ((), ()))
CONTRACT = (((0,), (0,)), ((), ()))


def place(step, gx, gy, sign):
    i, j, k, c = step % 4, (step // 4) % 4, (step // 16) % 4, step // 64
    dx = (2 * i + 3 * j + k + 2 * c) % 4
    dy = (3 * i + c) % 4
    dz = (2 * i + 3 * k + 2 * c) % 4
    if sign < 0:
        dx, dy, dz = 4 - dx, 4 - dy, 4 - dz
    x, y, z, core = gx // 4, gx % 4, gy // 2, gy % 2
    return ((x + dx) % 4) * 4 + (y + dy) % 4, ((z + dz) % 4) * 2 + (core + c) % 2


def kernel(
    slot_tok, slot_gate, pair_slot, pair_pos, pair_rank, gates, tok, og, wg_h, wu_h, wd_h,
    tg, gg, gwg_h, gwu_h, gwd_h,
    sbuf, rbuf, x2, s2, act, gp, gu, wg, wu, wd, back, flat, gsend, gback,
    local_sem, w_sem, out_sem, ssem, rsem, bssem, brsem, gssem, grsem,
):
    gx, gy = lax.axis_index("gx"), lax.axis_index("gy")
    to = functools.partial(place, gx=gx, gy=gy)
    barrier = pltpu.get_barrier_semaphore()

    def greet(p, _):
        pl.semaphore_signal(barrier, inc=1, device_id=to(p, sign=1), device_id_type=MESH)
        return 0

    lax.fori_loop(1, PEERS, greet, 0)
    loads = [pltpu.make_async_copy(h, v, w_sem.at[i]) for i, (h, v) in enumerate(((wg_h, wg), (wu_h, wu), (wd_h, wd)))]
    for load in loads:
        load.start()

    def gather(p, _):
        for s in range(CAP):
            t = slot_tok[p * CAP + s]
            sbuf[p, 0, s] = tok[t]
            sbuf[p, 1, s] = (og[t].astype(F32) * slot_gate[p * CAP + s]).astype(BF)
        return 0

    lax.fori_loop(0, PEERS, gather, 0)
    pl.semaphore_wait(barrier, PEERS - 1)
    own = pltpu.make_async_copy(sbuf.at[0], rbuf.at[0], local_sem.at[0])
    own.start()

    def send(p, _):
        for half in range(2):
            pltpu.make_async_remote_copy(
                sbuf.at[p, half], rbuf.at[p, half], ssem.at[p // PER], rsem.at[p // PER],
                device_id=to(p, sign=1), device_id_type=MESH,
            ).start()
        return 0

    lax.fori_loop(1, PEERS, send, 0)
    for load in loads:
        load.wait()
    own.wait()

    def span(buf, g):
        return buf.at[pl.ds(1, PER - 1)] if g == 0 else buf.at[pl.ds(g * PER, PER)]

    def rows_span(buf, g):
        return buf.at[pl.ds(CAP, ROWS - CAP)] if g == 0 else buf.at[pl.ds(g * ROWS, ROWS)]

    def whole(src, dst, a, b):
        return pltpu.make_async_remote_copy(src, dst, a, b, device_id=to(1, sign=1), device_id_type=MESH)

    lane = lax.broadcasted_iota(jnp.int32, (ROWS, 128), 1)
    row = lax.broadcasted_iota(jnp.int32, (ROWS, 128), 0)
    own_lane = lane == row % CAP
    sel = lax.broadcasted_iota(jnp.int32, (PER, ROWS), 0) == lax.broadcasted_iota(jnp.int32, (PER, ROWS), 1) // CAP
    sel = sel.astype(F32).astype(BF)

    for g in range(GROUPS):
        whole(span(sbuf, g), span(rbuf, g), ssem.at[g], rsem.at[g]).wait()
        here = pl.ds(g * ROWS, ROWS)
        for half, dst in ((0, x2), (1, s2)):

            def spread(c, _, half=half):
                part = rbuf[g * PER + c, half].reshape(CAP * TILES, 128).astype(F32)
                flat[pl.ds(pl.multiple_of(c * CAP * TILES, CAP * TILES), CAP * TILES), :] = part
                return 0

            lax.fori_loop(0, PER, spread, 0)
            for j in range(TILES):
                dst[here, j * 128 : (j + 1) * 128] = flat[pl.ds(j, ROWS, stride=TILES), :].astype(BF)

        def hidden(c, total):
            cols = pl.ds(pl.multiple_of(c * 256, 256), 256)
            pre_gate = jnp.dot(x2[here, :], wg[:, cols], preferred_element_type=F32)
            pre_up = jnp.dot(x2[here, :], wu[:, cols], preferred_element_type=F32)
            sback = lax.dot_general(s2[here, :], wd[cols, :], RIGHT, preferred_element_type=F32)
            sigma = jax.nn.sigmoid(pre_gate)
            silu = pre_gate * sigma
            a = (silu * pre_up).astype(BF)
            act[here, cols] = a
            gu[here, cols] = (sback * silu).astype(BF)
            gp[here, cols] = (sback * pre_up * sigma * (1.0 + pre_gate * (1.0 - sigma))).astype(BF)
            return total + jnp.sum(sback * a.astype(F32), axis=1, keepdims=True)

        total = lax.fori_loop(0, 3, hidden, jnp.zeros((ROWS, 1), F32))
        spread_gate = jnp.where(own_lane, total, 0.0).astype(BF)
        gate_rows = jnp.dot(sel, spread_gate, preferred_element_type=F32)
        for c in range(PER):
            gsend[g * PER + c] = gate_rows[c : c + 1, :]

        def inputs(n, _):
            rows = pl.ds(pl.multiple_of(n * 256, 256), 256)
            part = lax.dot_general(gp[here, :], wg[rows, :], RIGHT, preferred_element_type=F32)
            part += lax.dot_general(gu[here, :], wu[rows, :], RIGHT, preferred_element_type=F32)
            flat[pl.ds(2 * n, ROWS, stride=TILES), :] = part[:, :128]
            flat[pl.ds(2 * n + 1, ROWS, stride=TILES), :] = part[:, 128:]
            return 0

        lax.fori_loop(0, 8, inputs, 0)

        def pack(c, _):
            part = flat[pl.ds(pl.multiple_of(c * CAP * TILES, CAP * TILES), CAP * TILES), :]
            sbuf[g * PER + c, 0] = part.astype(BF).reshape(CAP, TILES, 128)
            return 0

        lax.fori_loop(0, PER, pack, 0)

        def give(p, _):
            device = to(p, sign=-1)
            pltpu.make_async_remote_copy(
                sbuf.at[p, 0], back.at[pl.ds(p * CAP, CAP)], bssem.at[g], brsem.at[g],
                device_id=device, device_id_type=MESH,
            ).start()
            pltpu.make_async_remote_copy(
                gsend.at[p], gback.at[p], gssem.at[g], grsem.at[g], device_id=device, device_id_type=MESH
            ).start()
            return 0

        if g == 0:
            own_back = pltpu.make_async_copy(sbuf.at[0, 0], back.at[pl.ds(0, CAP)], local_sem.at[0])
            own_gate = pltpu.make_async_copy(gsend.at[0], gback.at[0], local_sem.at[1])
            own_back.start()
            own_gate.start()
        lax.fori_loop(max(1, g * PER), (g + 1) * PER, give, 0)

    def w_in(n, _):
        rows = pl.ds(pl.multiple_of(n * 256, 256), 256)
        xt = x2[:, rows]
        wg[rows, :] = lax.dot_general(xt, gp[...], CONTRACT, preferred_element_type=F32).astype(BF)
        wu[rows, :] = lax.dot_general(xt, gu[...], CONTRACT, preferred_element_type=F32).astype(BF)
        return 0

    def w_out(n, _):
        rows = pl.ds(pl.multiple_of((n // 2) * 256, 256), 256)
        cols = pl.ds(pl.multiple_of((n % 2) * 1024, 1024), 1024)
        wd[rows, cols] = lax.dot_general(act[:, rows], s2[:, cols], CONTRACT, preferred_element_type=F32).astype(BF)
        return 0

    stores = [pltpu.make_async_copy(v, h, out_sem.at[i]) for i, (h, v) in enumerate(((gwg_h, wg), (gwu_h, wu), (gwd_h, wd)))]
    lax.fori_loop(0, 8, w_in, 0)
    stores[0].start()
    stores[1].start()
    lax.fori_loop(0, 6, w_out, 0)
    stores[2].start()

    own_back.wait()
    own_gate.wait()
    for g in range(GROUPS):
        first = 1 if g == 0 else 0
        src = sbuf.at[pl.ds(g * PER + first, PER - first), 0]
        whole(src, rows_span(back, g), bssem.at[g], brsem.at[g]).wait()
        whole(span(gsend, g), span(gback, g), gssem.at[g], grsem.at[g]).wait()

    def combine(t, _):
        total = back[pair_slot[t * 8]].astype(F32)
        for k in range(1, 8):
            total += back[pair_slot[t * 8 + k]].astype(F32)
        tg[t] = total.astype(BF)
        return 0

    lax.fori_loop(0, 128, combine, 0)
    table = gback[...].reshape(PEERS, 128).astype(BF)
    lanes = lax.broadcasted_iota(jnp.int32, (128, 128), 1)
    lane8 = lax.broadcasted_iota(jnp.int32, (128, 8), 1)
    result = jnp.zeros((128, 8), F32)
    for k in range(8):
        pick = (lanes == pair_pos[:, k : k + 1]).astype(F32).astype(BF)
        found = jnp.dot(pick, table, preferred_element_type=F32)
        value = jnp.sum(jnp.where(lanes == pair_rank[:, k : k + 1], found, 0.0), axis=1, keepdims=True)
        result = jnp.where(lane8 == k, value, result)
    gg[...] = (result / gates[...].astype(F32)).astype(BF)
    for store in stores:
        store.wait()


def on_device(tokens, out_grad, expert_ids, gate_weights, w_gate, w_up, w_down):
    gx, gy = lax.axis_index("gx"), lax.axis_index("gy")
    tok, top = expert_ids.shape
    width, ff = w_gate.shape[1:]
    steps = jnp.arange(PEERS, dtype=jnp.int32)
    px, py = place(steps, gx, gy, 1)
    named = (expert_ids[:, :, None] == (px * 8 + py)).astype(F32)
    member = jnp.sum(named, axis=1)
    gate_of = jnp.sum(named * gate_weights.astype(F32)[:, :, None], axis=1)
    earlier = (jnp.arange(tok)[:, None] > jnp.arange(tok)[None, :]).astype(BF)
    rank = jnp.dot(earlier, member.astype(BF), preferred_element_type=F32)
    pair_pos = jnp.sum(named * steps.astype(F32), axis=2).astype(jnp.int32)
    pair_rank = jnp.sum(named * rank[:, None, :], axis=2).astype(jnp.int32)
    pair_slot = (pair_pos * CAP + pair_rank).reshape(tok * top)
    at = jnp.where(member > 0, rank, -1.0).T
    pick = (at[:, None, :] == jnp.arange(CAP, dtype=F32)[None, :, None]).astype(F32)
    slot_tok = jnp.sum(pick * jnp.arange(tok, dtype=F32), axis=2).astype(jnp.int32)
    slot_gate = jnp.sum(pick * gate_of.T[:, None, :], axis=2)

    smem, vmem, hbm = (pl.BlockSpec(memory_space=m) for m in (pltpu.SMEM, pltpu.VMEM, pl.ANY))
    dma = pltpu.SemaphoreType.DMA
    tg, gg, gwg, gwu, gwd = pl.pallas_call(
        kernel,
        out_shape=(
            jax.ShapeDtypeStruct((tok, TILES, 128), BF),
            jax.ShapeDtypeStruct((tok, top), BF),
            jax.ShapeDtypeStruct((width, ff), BF),
            jax.ShapeDtypeStruct((width, ff), BF),
            jax.ShapeDtypeStruct((ff, width), BF),
        ),
        in_specs=[smem] * 3 + [vmem] * 5 + [hbm] * 3,
        out_specs=(vmem, vmem, hbm, hbm, hbm),
        scratch_shapes=[
            pltpu.VMEM((PEERS, 2, CAP, TILES, 128), BF),
            pltpu.VMEM((PEERS, 2, CAP, TILES, 128), BF),
            pltpu.VMEM((PEERS * CAP, width), BF),
            pltpu.VMEM((PEERS * CAP, width), BF),
            pltpu.VMEM((PEERS * CAP, ff), BF),
            pltpu.VMEM((PEERS * CAP, ff), BF),
            pltpu.VMEM((PEERS * CAP, ff), BF),
            pltpu.VMEM((width, ff), BF),
            pltpu.VMEM((width, ff), BF),
            pltpu.VMEM((ff, width), BF),
            pltpu.VMEM((PEERS * CAP, TILES, 128), BF),
            pltpu.VMEM((ROWS * TILES, 128), F32),
            pltpu.VMEM((PEERS, 1, 128), F32),
            pltpu.VMEM((PEERS, 1, 128), F32),
            dma((2,)),
            dma((3,)),
            dma((3,)),
            dma((GROUPS,)),
            dma((GROUPS,)),
            dma((GROUPS,)),
            dma((GROUPS,)),
            dma((GROUPS,)),
            dma((GROUPS,)),
        ],
        compiler_params=pltpu.CompilerParams(collective_id=0, has_side_effects=True, vmem_limit_bytes=60 << 20),
        cost_estimate=pl.CostEstimate(flops=29 * 10**9, bytes_accessed=20 * 10**6, transcendentals=10**6),
        name="routed_backward",
    )(
        slot_tok.reshape(-1),
        slot_gate.reshape(-1),
        pair_slot,
        pair_pos,
        pair_rank,
        gate_weights,
        tokens.reshape(tok, TILES, 128),
        out_grad.reshape(tok, TILES, 128),
        w_gate[0],
        w_up[0],
        w_down[0],
    )
    return (tg.reshape(tok, width), gg, gwg[None], gwu[None], gwd[None])


def solution(mesh):
    both = ("gx", "gy")
    return jax.shard_map(
        on_device,
        mesh=mesh,
        in_specs=(P(both, None),) * 4 + (P(both, None, None),) * 3,
        out_specs=(P(both, None),) * 2 + (P(both, None, None),) * 3,
        check_vma=False,
    )
```

```python
import functools

import jax
import jax.numpy as jnp
from jax import lax
from jax.experimental import pallas as pl
from jax.experimental.pallas import tpu as pltpu
from jax.sharding import PartitionSpec as P

BF = jnp.bfloat16
F32 = jnp.float32
PEERS = 128
CAP = 9
GROUPS = 4
PER = PEERS // GROUPS
ROWS = PER * CAP
TILES = 16
MESH = pl.DeviceIdType.MESH
RIGHT = (((1,), (1,)), ((), ()))
CONTRACT = (((0,), (0,)), ((), ()))


def place(step, gx, gy, sign):
    i, j, k, c = lax.rem(step, 4), lax.rem(lax.div(step, 4), 4), lax.rem(lax.div(step, 16), 4), lax.div(step, 64)
    dx = 2 * i + 3 * j + k + 2 * c
    dy = 3 * i + c
    dz = 2 * i + 3 * k + 2 * c
    x, y, z, core = lax.div(gx, 4), lax.rem(gx, 4), lax.div(gy, 2), lax.rem(gy, 2)
    if sign < 0:
        dx, dy, dz = 32 - dx, 32 - dy, 32 - dz
    return lax.rem(x + dx, 4) * 4 + lax.rem(y + dy, 4), lax.rem(z + dz, 4) * 2 + lax.rem(core + c, 2)


def kernel(
    ids, gates, tok, og, wg_h, wu_h, wd_h,
    tg, gg, gwg_h, gwu_h, gwd_h,
    sbuf, rbuf, x2, s2, act, gp, gu, wg, wu, wd, back, flat, gsend, gback,
    tokt, ogt, ranks, tok_v, gate_v, pair_v, slot_tok, slot_gate, pair_slot, table_sem,
    local_sem, w_sem, out_sem, ssem, rsem, bssem, brsem, gssem, grsem,
):
    gx, gy = lax.axis_index("gx"), lax.axis_index("gy")
    to = functools.partial(place, gx=gx, gy=gy)
    barrier = pltpu.get_barrier_semaphore()

    def greet(p, _):
        pl.semaphore_signal(barrier, inc=1, device_id=to(p, sign=1), device_id_type=MESH)
        return 0

    lax.fori_loop(1, PEERS, greet, 0)
    loads = [pltpu.make_async_copy(h, v, w_sem.at[i]) for i, (h, v) in enumerate(((wg_h, wg), (wu_h, wu), (wd_h, wd)))]
    for load in loads:
        load.start()

    step_of = lax.broadcasted_iota(jnp.int32, (PEERS, 128), 0)
    tok_of = lax.broadcasted_iota(jnp.int32, (PEERS, 128), 1)
    ex, ey = to(step_of, sign=1)
    expert = ex * 8 + ey

    def named(k):
        return (expert == ids[k : k + 1, :]).astype(F32)

    gate_rows8 = gates[...].astype(F32)
    member = jnp.zeros((PEERS, 128), F32)
    gate_of = jnp.zeros((PEERS, 128), F32)
    for k in range(8):
        member += named(k)
        gate_of += named(k) * gate_rows8[k : k + 1, :]
    earlier = (step_of < tok_of).astype(F32).astype(BF)
    rank = jnp.dot(member.astype(BF), earlier, preferred_element_type=F32)
    ranks[...] = rank
    toks = jnp.zeros((PEERS, 128), F32)
    slot_gates = jnp.zeros((PEERS, 128), F32)
    tok_f = tok_of.astype(F32)
    for s in range(CAP):
        pick = jnp.where(rank == s, member, 0.0)
        toks = jnp.where(tok_of == s, jnp.sum(pick * tok_f, axis=1, keepdims=True), toks)
        slot_gates = jnp.where(tok_of == s, jnp.sum(pick * gate_of, axis=1, keepdims=True), slot_gates)
    tok_v[...] = jnp.clip(toks.astype(jnp.int32), 0, 127)
    gate_v[...] = slot_gates
    slots = step_of.astype(F32) * CAP + rank
    for k in range(8):
        slot = jnp.sum(named(k) * slots, axis=0, keepdims=True).astype(jnp.int32)
        pair_v[k : k + 1, :] = jnp.clip(slot, 0, PEERS * CAP - 1)
    tables = [
        pltpu.make_async_copy(v, m, table_sem.at[i])
        for i, (v, m) in enumerate(((tok_v, slot_tok), (gate_v, slot_gate), (pair_v, pair_slot)))
    ]
    for table in tables:
        table.start()
    for src, dst in ((tok, tokt), (og, ogt)):
        for j in range(TILES):
            flat[pl.ds(j, 128, stride=TILES), :] = src[:, j * 128 : (j + 1) * 128].astype(F32)

        def tile(c, _, dst=dst):
            part = flat[pl.ds(pl.multiple_of(c * 8 * TILES, 8 * TILES), 8 * TILES), :]
            dst[pl.ds(pl.multiple_of(c * 8, 8), 8)] = part.astype(BF).reshape(8, TILES, 128)
            return 0

        lax.fori_loop(0, 16, tile, 0)
    for table in tables:
        table.wait()

    def gather_x(p, _):
        for s in range(CAP):
            sbuf[p, 0, s] = tokt[slot_tok[p, s]]
        return 0

    def gather_dy(p, _):
        for s in range(CAP):
            sbuf[p, 1, s] = (ogt[slot_tok[p, s]].astype(F32) * slot_gate[p, s]).astype(BF)
        return 0

    def send(p, _, half, g):
        pltpu.make_async_remote_copy(
            sbuf.at[p, half], rbuf.at[p, half], ssem.at[g], rsem.at[g],
            device_id=to(p, sign=1), device_id_type=MESH,
        ).start()
        return 0

    for g in range(GROUPS):
        lo, hi = g * PER, (g + 1) * PER
        lax.fori_loop(lo, hi, gather_x, 0)
        if g == 0:
            pl.semaphore_wait(barrier, PEERS - 1)
        lax.fori_loop(max(1, lo), hi, functools.partial(send, half=0, g=g), 0)
        lax.fori_loop(lo, hi, gather_dy, 0)
        lax.fori_loop(max(1, lo), hi, functools.partial(send, half=1, g=g), 0)
    own = pltpu.make_async_copy(sbuf.at[0], rbuf.at[0], local_sem.at[0])
    own.start()
    for load in loads:
        load.wait()
    own.wait()

    def span(buf, g):
        return buf.at[pl.ds(1, PER - 1)] if g == 0 else buf.at[pl.ds(g * PER, PER)]

    def rows_span(buf, g):
        return buf.at[pl.ds(CAP, ROWS - CAP)] if g == 0 else buf.at[pl.ds(g * ROWS, ROWS)]

    def whole(src, dst, a, b):
        return pltpu.make_async_remote_copy(src, dst, a, b, device_id=to(1, sign=1), device_id_type=MESH)

    lane = lax.broadcasted_iota(jnp.int32, (ROWS, 128), 1)
    row = lax.broadcasted_iota(jnp.int32, (ROWS, 128), 0)
    own_lane = lane == row % CAP
    sel = lax.broadcasted_iota(jnp.int32, (PER, ROWS), 0) == lax.broadcasted_iota(jnp.int32, (PER, ROWS), 1) // CAP
    sel = sel.astype(F32).astype(BF)

    for g in range(GROUPS):
        whole(span(sbuf, g), span(rbuf, g), ssem.at[g], rsem.at[g]).wait()
        here = pl.ds(g * ROWS, ROWS)
        for half, dst in ((0, x2), (1, s2)):

            def spread(c, _, half=half):
                part = rbuf[g * PER + c, half].reshape(CAP * TILES, 128).astype(F32)
                flat[pl.ds(pl.multiple_of(c * CAP * TILES, CAP * TILES), CAP * TILES), :] = part
                return 0

            lax.fori_loop(0, PER, spread, 0)
            for j in range(TILES):
                dst[here, j * 128 : (j + 1) * 128] = flat[pl.ds(j, ROWS, stride=TILES), :].astype(BF)

        def hidden(c, total):
            cols = pl.ds(pl.multiple_of(c * 256, 256), 256)
            pre_gate = jnp.dot(x2[here, :], wg[:, cols], preferred_element_type=F32)
            pre_up = jnp.dot(x2[here, :], wu[:, cols], preferred_element_type=F32)
            sback = lax.dot_general(s2[here, :], wd[cols, :], RIGHT, preferred_element_type=F32)
            sigma = jax.nn.sigmoid(pre_gate)
            silu = pre_gate * sigma
            a = (silu * pre_up).astype(BF)
            act[here, cols] = a
            gu[here, cols] = (sback * silu).astype(BF)
            gp[here, cols] = (sback * pre_up * sigma * (1.0 + pre_gate * (1.0 - sigma))).astype(BF)
            return total + jnp.sum(sback * a.astype(F32), axis=1, keepdims=True)

        total = lax.fori_loop(0, 3, hidden, jnp.zeros((ROWS, 1), F32))
        spread_gate = jnp.where(own_lane, total, 0.0).astype(BF)
        gate_rows = jnp.dot(sel, spread_gate, preferred_element_type=F32)
        for c in range(PER):
            gsend[g * PER + c] = gate_rows[c : c + 1, :]

        def inputs(n, _):
            rows = pl.ds(pl.multiple_of(n * 256, 256), 256)
            part = lax.dot_general(gp[here, :], wg[rows, :], RIGHT, preferred_element_type=F32)
            part += lax.dot_general(gu[here, :], wu[rows, :], RIGHT, preferred_element_type=F32)
            flat[pl.ds(2 * n, ROWS, stride=TILES), :] = part[:, :128]
            flat[pl.ds(2 * n + 1, ROWS, stride=TILES), :] = part[:, 128:]
            return 0

        lax.fori_loop(0, 8, inputs, 0)

        def pack(c, _):
            part = flat[pl.ds(pl.multiple_of(c * CAP * TILES, CAP * TILES), CAP * TILES), :]
            sbuf[g * PER + c, 0] = part.astype(BF).reshape(CAP, TILES, 128)
            return 0

        lax.fori_loop(0, PER, pack, 0)

        def give(p, _):
            device = to(p, sign=-1)
            pltpu.make_async_remote_copy(
                sbuf.at[p, 0], back.at[pl.ds(p * CAP, CAP)], bssem.at[g], brsem.at[g],
                device_id=device, device_id_type=MESH,
            ).start()
            pltpu.make_async_remote_copy(
                gsend.at[p], gback.at[p], gssem.at[g], grsem.at[g], device_id=device, device_id_type=MESH
            ).start()
            return 0

        if g == 0:
            own_back = pltpu.make_async_copy(sbuf.at[0, 0], back.at[pl.ds(0, CAP)], local_sem.at[0])
            own_gate = pltpu.make_async_copy(gsend.at[0], gback.at[0], local_sem.at[1])
            own_back.start()
            own_gate.start()
        lax.fori_loop(max(1, g * PER), (g + 1) * PER, give, 0)

    def w_in(n, _):
        rows = pl.ds(pl.multiple_of(n * 256, 256), 256)
        xt = x2[:, rows]
        wg[rows, :] = lax.dot_general(xt, gp[...], CONTRACT, preferred_element_type=F32).astype(BF)
        wu[rows, :] = lax.dot_general(xt, gu[...], CONTRACT, preferred_element_type=F32).astype(BF)
        return 0

    def w_out(n, _):
        rows = pl.ds(pl.multiple_of((n // 2) * 256, 256), 256)
        cols = pl.ds(pl.multiple_of((n % 2) * 1024, 1024), 1024)
        wd[rows, cols] = lax.dot_general(act[:, rows], s2[:, cols], CONTRACT, preferred_element_type=F32).astype(BF)
        return 0

    stores = [pltpu.make_async_copy(v, h, out_sem.at[i]) for i, (h, v) in enumerate(((gwg_h, wg), (gwu_h, wu), (gwd_h, wd)))]
    lax.fori_loop(0, 8, w_in, 0)
    stores[0].start()
    stores[1].start()
    lax.fori_loop(0, 6, w_out, 0)
    stores[2].start()

    own_back.wait()
    own_gate.wait()
    for g in range(GROUPS):
        first = 1 if g == 0 else 0
        src = sbuf.at[pl.ds(g * PER + first, PER - first), 0]
        whole(src, rows_span(back, g), bssem.at[g], brsem.at[g]).wait()
        whole(span(gsend, g), span(gback, g), gssem.at[g], grsem.at[g]).wait()

    def combine(t, _):
        total = back[pair_slot[0, t]].astype(F32)
        for k in range(1, 8):
            total += back[pair_slot[k, t]].astype(F32)
        flat[pl.ds(pl.multiple_of(t * TILES, TILES), TILES), :] = total
        return 0

    lax.fori_loop(0, 128, combine, 0)
    for j in range(TILES):
        tg[:, j * 128 : (j + 1) * 128] = flat[pl.ds(j, 128, stride=TILES), :].astype(BF)
    table = gback[...].reshape(PEERS, 128)
    rank = ranks[...]
    found = jnp.zeros((PEERS, 128), F32)
    for s in range(CAP):
        found = jnp.where(rank == s, table[:, s : s + 1], found)
    ex, ey = to(step_of, sign=1)
    expert = ex * 8 + ey
    for k in range(8):
        value = jnp.sum((expert == ids[k : k + 1, :]).astype(F32) * found, axis=0, keepdims=True)
        gg[k : k + 1, :] = (value / gates[k : k + 1, :].astype(F32)).astype(BF)
    for store in stores:
        store.wait()


def on_device(tokens, out_grad, expert_ids, gate_weights, w_gate, w_up, w_down):
    tok, top = expert_ids.shape
    width, ff = w_gate.shape[1:]
    vmem, hbm = pl.BlockSpec(memory_space=pltpu.VMEM), pl.BlockSpec(memory_space=pl.ANY)
    dma = pltpu.SemaphoreType.DMA
    tg, gg, gwg, gwu, gwd = pl.pallas_call(
        kernel,
        out_shape=(
            jax.ShapeDtypeStruct((tok, width), BF),
            jax.ShapeDtypeStruct((top, tok), BF),
            jax.ShapeDtypeStruct((width, ff), BF),
            jax.ShapeDtypeStruct((width, ff), BF),
            jax.ShapeDtypeStruct((ff, width), BF),
        ),
        in_specs=[vmem] * 4 + [hbm] * 3,
        out_specs=(vmem, vmem, hbm, hbm, hbm),
        scratch_shapes=[
            pltpu.VMEM((PEERS, 2, CAP, TILES, 128), BF),
            pltpu.VMEM((PEERS, 2, CAP, TILES, 128), BF),
            pltpu.VMEM((PEERS * CAP, width), BF),
            pltpu.VMEM((PEERS * CAP, width), BF),
            pltpu.VMEM((PEERS * CAP, ff), BF),
            pltpu.VMEM((PEERS * CAP, ff), BF),
            pltpu.VMEM((PEERS * CAP, ff), BF),
            pltpu.VMEM((width, ff), BF),
            pltpu.VMEM((width, ff), BF),
            pltpu.VMEM((ff, width), BF),
            pltpu.VMEM((PEERS * CAP, TILES, 128), BF),
            pltpu.VMEM((ROWS * TILES, 128), F32),
            pltpu.VMEM((PEERS, 1, 128), F32),
            pltpu.VMEM((PEERS, 1, 128), F32),
            pltpu.VMEM((tok, TILES, 128), BF),
            pltpu.VMEM((tok, TILES, 128), BF),
            pltpu.VMEM((PEERS, tok), F32),
            pltpu.VMEM((PEERS, 128), jnp.int32),
            pltpu.VMEM((PEERS, 128), F32),
            pltpu.VMEM((top, tok), jnp.int32),
            pltpu.SMEM((PEERS, 128), jnp.int32),
            pltpu.SMEM((PEERS, 128), F32),
            pltpu.SMEM((top, tok), jnp.int32),
            dma((3,)),
            dma((2,)),
            dma((3,)),
            dma((3,)),
            dma((GROUPS,)),
            dma((GROUPS,)),
            dma((GROUPS,)),
            dma((GROUPS,)),
            dma((GROUPS,)),
            dma((GROUPS,)),
        ],
        compiler_params=pltpu.CompilerParams(collective_id=0, has_side_effects=True, vmem_limit_bytes=60 << 20),
        cost_estimate=pl.CostEstimate(flops=29 * 10**9, bytes_accessed=20 * 10**6, transcendentals=10**6),
        name="routed_backward",
    )(
        expert_ids.T,
        gate_weights.T,
        tokens,
        out_grad,
        w_gate[0],
        w_up[0],
        w_down[0],
    )
    return (tg, gg.T, gwg[None], gwu[None], gwd[None])


def solution(mesh):
    both = ("gx", "gy")
    return jax.shard_map(
        on_device,
        mesh=mesh,
        in_specs=(P(both, None),) * 4 + (P(both, None, None),) * 3,
        out_specs=(P(both, None),) * 2 + (P(both, None, None),) * 3,
        check_vma=False,
    )
```

```python
import functools

import jax
import jax.numpy as jnp
from jax import lax
from jax.experimental import pallas as pl
from jax.experimental.pallas import tpu as pltpu
from jax.sharding import PartitionSpec as P

BF = jnp.bfloat16
F32 = jnp.float32
PEERS = 128
CAP = 9
GROUPS = 4
PARTS = 3
PART = CAP // PARTS
PER = PEERS // GROUPS
ROWS = PER * CAP
TILES = 16
MESH = pl.DeviceIdType.MESH
RIGHT = (((1,), (1,)), ((), ()))
CONTRACT = (((0,), (0,)), ((), ()))


def place(step, gx, gy, sign):
    i, j, k, c = lax.rem(step, 4), lax.rem(lax.div(step, 4), 4), lax.rem(lax.div(step, 16), 4), lax.div(step, 64)
    dx = 2 * i + 3 * j + k + 2 * c
    dy = 3 * i + c
    dz = 2 * i + 3 * k + 2 * c
    x, y, z, core = lax.div(gx, 4), lax.rem(gx, 4), lax.div(gy, 2), lax.rem(gy, 2)
    if sign < 0:
        dx, dy, dz = 32 - dx, 32 - dy, 32 - dz
    return lax.rem(x + dx, 4) * 4 + lax.rem(y + dy, 4), lax.rem(z + dz, 4) * 2 + lax.rem(core + c, 2)


def each(g, gx, gy, sign, act):
    x, y, z, core = lax.div(gx, 4), lax.rem(gx, 4), lax.div(gy, 2), lax.rem(gy, 2)
    c = g // 2
    other = lax.rem(core + c, 2)
    ys = [lax.rem(y + (3 * i + c if sign > 0 else 16 - 3 * i - c), 4) for i in range(4)]

    def serve(m, first):
        j, k = lax.rem(m, 4), lax.div(m, 4) + 2 * (g % 2)
        dx = 3 * j + k + 2 * c
        dz = 3 * k + 2 * c
        bx, bz = (x + dx, z + dz) if sign > 0 else (x + 32 - dx, z + 32 - dz)
        even = lax.rem(bx, 4) * 4, lax.rem(bz, 4) * 2 + other
        odd = lax.rem(bx + 2, 4) * 4, lax.rem(bz + 2, 4) * 2 + other
        for i in range(first, 4):
            a, b = odd if i % 2 else even
            act(g * PER + m * 4 + i, (a + ys[i], b))

    if g == 0:
        serve(jnp.int32(0), 1)

    def step(m, _):
        serve(m, 0)
        return 0

    lax.fori_loop(1 if g == 0 else 0, PER // 4, step, 0)


def kernel(
    ids, gates, tok, og, wg_h, wu_h, wd_h,
    tg, gg, gwg_h, gwu_h, gwd_h,
    sbuf, rbuf, x2, s2, act, gp, gu, wg, wu, wd, back, flat, gsend, gback,
    tokt, ogt, ranks, tok_v, gate_v, pair_v, slot_tok, slot_gate, pair_slot, table_sem,
    local_sem, w_sem, out_sem, ssem, rsem, bssem, brsem, gssem, grsem,
):
    gx, gy = lax.axis_index("gx"), lax.axis_index("gy")
    to = functools.partial(place, gx=gx, gy=gy)
    barrier = pltpu.get_barrier_semaphore()

    def greet(p, device):
        pl.semaphore_signal(barrier, inc=1, device_id=device, device_id_type=MESH)

    for g in range(GROUPS):
        each(g, gx, gy, 1, greet)
    loads = [pltpu.make_async_copy(h, v, w_sem.at[i]) for i, (h, v) in enumerate(((wg_h, wg), (wu_h, wu), (wd_h, wd)))]
    for load in loads:
        load.start()

    step_of = lax.broadcasted_iota(jnp.int32, (PEERS, 128), 0)
    tok_of = lax.broadcasted_iota(jnp.int32, (PEERS, 128), 1)
    ex, ey = to(step_of, sign=1)
    expert = ex * 8 + ey

    def named(k):
        return (expert == ids[k : k + 1, :]).astype(F32)

    gate_rows8 = gates[...].astype(F32)
    member = jnp.zeros((PEERS, 128), F32)
    gate_of = jnp.zeros((PEERS, 128), F32)
    for k in range(8):
        member += named(k)
        gate_of += named(k) * gate_rows8[k : k + 1, :]
    earlier = (step_of < tok_of).astype(F32).astype(BF)
    rank = jnp.dot(member.astype(BF), earlier, preferred_element_type=F32)
    ranks[...] = rank
    toks = jnp.zeros((PEERS, 128), F32)
    slot_gates = jnp.zeros((PEERS, 128), F32)
    tok_f = tok_of.astype(F32)
    for s in range(CAP):
        pick = jnp.where(rank == s, member, 0.0)
        toks = jnp.where(tok_of == s, jnp.sum(pick * tok_f, axis=1, keepdims=True), toks)
        slot_gates = jnp.where(tok_of == s, jnp.sum(pick * gate_of, axis=1, keepdims=True), slot_gates)
    tok_v[...] = jnp.clip(toks.astype(jnp.int32), 0, 127)
    gate_v[...] = slot_gates
    slots = step_of.astype(F32) * CAP + rank
    for k in range(8):
        slot = jnp.sum(named(k) * slots, axis=0, keepdims=True).astype(jnp.int32)
        pair_v[k : k + 1, :] = jnp.clip(slot, 0, PEERS * CAP - 1)
    tables = [
        pltpu.make_async_copy(v, m, table_sem.at[i])
        for i, (v, m) in enumerate(((tok_v, slot_tok), (gate_v, slot_gate), (pair_v, pair_slot)))
    ]
    for table in tables:
        table.start()
    for src, dst in ((tok, tokt), (og, ogt)):
        for j in range(TILES):
            flat[pl.ds(j, 128, stride=TILES), :] = src[:, j * 128 : (j + 1) * 128].astype(F32)

        def tile(c, _, dst=dst):
            part = flat[pl.ds(pl.multiple_of(c * 8 * TILES, 8 * TILES), 8 * TILES), :]
            dst[pl.ds(pl.multiple_of(c * 8, 8), 8)] = part.astype(BF).reshape(8, TILES, 128)
            return 0

        lax.fori_loop(0, 16, tile, 0)
    for table in tables:
        table.wait()

    def gather_x(p, _):
        for s in range(CAP):
            sbuf[p, 0, s] = tokt[slot_tok[p, s]]
        return 0

    def gather_dy(p, _):
        for s in range(CAP):
            sbuf[p, 1, s] = (ogt[slot_tok[p, s]].astype(F32) * slot_gate[p, s]).astype(BF)
        return 0

    def send(p, device, half, g, part):
        rows = pl.ds(part * PART, PART)
        pltpu.make_async_remote_copy(
            sbuf.at[p, half, rows], rbuf.at[p, half, rows], ssem.at[g], rsem.at[g],
            device_id=device, device_id_type=MESH,
        ).start()

    for g in range(GROUPS):
        lo, hi = g * PER, (g + 1) * PER
        lax.fori_loop(lo, hi, gather_x, 0)
        if g == 0:
            pl.semaphore_wait(barrier, PEERS - 1)
        for part in range(PARTS):
            each(g, gx, gy, 1, functools.partial(send, half=0, g=g, part=part))
        lax.fori_loop(lo, hi, gather_dy, 0)
        for part in range(PARTS):
            each(g, gx, gy, 1, functools.partial(send, half=1, g=g, part=part))
    own = pltpu.make_async_copy(sbuf.at[0], rbuf.at[0], local_sem.at[0])
    own.start()
    for load in loads:
        load.wait()
    own.wait()

    def span(buf, g):
        return buf.at[pl.ds(1, PER - 1)] if g == 0 else buf.at[pl.ds(g * PER, PER)]

    def rows_span(buf, g):
        return buf.at[pl.ds(CAP, ROWS - CAP)] if g == 0 else buf.at[pl.ds(g * ROWS, ROWS)]

    def whole(src, dst, a, b):
        return pltpu.make_async_remote_copy(src, dst, a, b, device_id=to(1, sign=1), device_id_type=MESH)

    lane = lax.broadcasted_iota(jnp.int32, (ROWS, 128), 1)
    row = lax.broadcasted_iota(jnp.int32, (ROWS, 128), 0)
    own_lane = lane == row % CAP
    sel = lax.broadcasted_iota(jnp.int32, (PER, ROWS), 0) == lax.broadcasted_iota(jnp.int32, (PER, ROWS), 1) // CAP
    sel = sel.astype(F32).astype(BF)

    for g in range(GROUPS):
        whole(span(sbuf, g), span(rbuf, g), ssem.at[g], rsem.at[g]).wait()
        here = pl.ds(g * ROWS, ROWS)
        for half, dst in ((0, x2), (1, s2)):

            def spread(c, _, half=half):
                part = rbuf[g * PER + c, half].reshape(CAP * TILES, 128).astype(F32)
                flat[pl.ds(pl.multiple_of(c * CAP * TILES, CAP * TILES), CAP * TILES), :] = part
                return 0

            lax.fori_loop(0, PER, spread, 0)
            for j in range(TILES):
                dst[here, j * 128 : (j + 1) * 128] = flat[pl.ds(j, ROWS, stride=TILES), :].astype(BF)

        def hidden(c, total):
            cols = pl.ds(pl.multiple_of(c * 256, 256), 256)
            pre_gate = jnp.dot(x2[here, :], wg[:, cols], preferred_element_type=F32)
            pre_up = jnp.dot(x2[here, :], wu[:, cols], preferred_element_type=F32)
            sback = lax.dot_general(s2[here, :], wd[cols, :], RIGHT, preferred_element_type=F32)
            sigma = jax.nn.sigmoid(pre_gate)
            silu = pre_gate * sigma
            a = (silu * pre_up).astype(BF)
            act[here, cols] = a
            gu[here, cols] = (sback * silu).astype(BF)
            gp[here, cols] = (sback * pre_up * sigma * (1.0 + pre_gate * (1.0 - sigma))).astype(BF)
            return total + jnp.sum(sback * a.astype(F32), axis=1, keepdims=True)

        total = lax.fori_loop(0, 3, hidden, jnp.zeros((ROWS, 1), F32))
        spread_gate = jnp.where(own_lane, total, 0.0).astype(BF)
        gate_rows = jnp.dot(sel, spread_gate, preferred_element_type=F32)
        for c in range(PER):
            gsend[g * PER + c] = gate_rows[c : c + 1, :]

        def inputs(n, _):
            rows = pl.ds(pl.multiple_of(n * 256, 256), 256)
            part = lax.dot_general(gp[here, :], wg[rows, :], RIGHT, preferred_element_type=F32)
            part += lax.dot_general(gu[here, :], wu[rows, :], RIGHT, preferred_element_type=F32)
            flat[pl.ds(2 * n, ROWS, stride=TILES), :] = part[:, :128]
            flat[pl.ds(2 * n + 1, ROWS, stride=TILES), :] = part[:, 128:]
            return 0

        lax.fori_loop(0, 8, inputs, 0)

        def pack(c, _):
            part = flat[pl.ds(pl.multiple_of(c * CAP * TILES, CAP * TILES), CAP * TILES), :]
            sbuf[g * PER + c, 0] = part.astype(BF).reshape(CAP, TILES, 128)
            return 0

        lax.fori_loop(0, PER, pack, 0)

        def give(p, device, part):
            pltpu.make_async_remote_copy(
                sbuf.at[p, 0, pl.ds(part * PART, PART)], back.at[pl.ds(p * CAP + part * PART, PART)],
                bssem.at[g], brsem.at[g], device_id=device, device_id_type=MESH,
            ).start()

        def give_gate(p, device):
            pltpu.make_async_remote_copy(
                gsend.at[p], gback.at[p], gssem.at[g], grsem.at[g], device_id=device, device_id_type=MESH
            ).start()

        if g == 0:
            own_back = pltpu.make_async_copy(sbuf.at[0, 0], back.at[pl.ds(0, CAP)], local_sem.at[0])
            own_gate = pltpu.make_async_copy(gsend.at[0], gback.at[0], local_sem.at[1])
            own_back.start()
            own_gate.start()
        for part in range(PARTS):
            each(g, gx, gy, -1, functools.partial(give, part=part))
        each(g, gx, gy, -1, give_gate)

    def w_in(n, _):
        rows = pl.ds(pl.multiple_of(n * 256, 256), 256)
        xt = x2[:, rows]
        wg[rows, :] = lax.dot_general(xt, gp[...], CONTRACT, preferred_element_type=F32).astype(BF)
        wu[rows, :] = lax.dot_general(xt, gu[...], CONTRACT, preferred_element_type=F32).astype(BF)
        return 0

    def w_out(n, _):
        rows = pl.ds(pl.multiple_of((n // 2) * 256, 256), 256)
        cols = pl.ds(pl.multiple_of((n % 2) * 1024, 1024), 1024)
        wd[rows, cols] = lax.dot_general(act[:, rows], s2[:, cols], CONTRACT, preferred_element_type=F32).astype(BF)
        return 0

    stores = [pltpu.make_async_copy(v, h, out_sem.at[i]) for i, (h, v) in enumerate(((gwg_h, wg), (gwu_h, wu), (gwd_h, wd)))]
    lax.fori_loop(0, 8, w_in, 0)
    stores[0].start()
    stores[1].start()
    lax.fori_loop(0, 6, w_out, 0)
    stores[2].start()

    own_back.wait()
    own_gate.wait()
    for g in range(GROUPS):
        first = 1 if g == 0 else 0
        src = sbuf.at[pl.ds(g * PER + first, PER - first), 0]
        whole(src, rows_span(back, g), bssem.at[g], brsem.at[g]).wait()
        whole(span(gsend, g), span(gback, g), gssem.at[g], grsem.at[g]).wait()

    def combine(t, _):
        total = back[pair_slot[0, t]].astype(F32)
        for k in range(1, 8):
            total += back[pair_slot[k, t]].astype(F32)
        flat[pl.ds(pl.multiple_of(t * TILES, TILES), TILES), :] = total
        return 0

    lax.fori_loop(0, 128, combine, 0)
    for j in range(TILES):
        tg[:, j * 128 : (j + 1) * 128] = flat[pl.ds(j, 128, stride=TILES), :].astype(BF)
    table = gback[...].reshape(PEERS, 128)
    rank = ranks[...]
    found = jnp.zeros((PEERS, 128), F32)
    for s in range(CAP):
        found = jnp.where(rank == s, table[:, s : s + 1], found)
    ex, ey = to(step_of, sign=1)
    expert = ex * 8 + ey
    for k in range(8):
        value = jnp.sum((expert == ids[k : k + 1, :]).astype(F32) * found, axis=0, keepdims=True)
        gg[k : k + 1, :] = (value / gates[k : k + 1, :].astype(F32)).astype(BF)
    for store in stores:
        store.wait()


def on_device(tokens, out_grad, expert_ids, gate_weights, w_gate, w_up, w_down):
    tok, top = expert_ids.shape
    width, ff = w_gate.shape[1:]
    vmem, hbm = pl.BlockSpec(memory_space=pltpu.VMEM), pl.BlockSpec(memory_space=pl.ANY)
    dma = pltpu.SemaphoreType.DMA
    tg, gg, gwg, gwu, gwd = pl.pallas_call(
        kernel,
        out_shape=(
            jax.ShapeDtypeStruct((tok, width), BF),
            jax.ShapeDtypeStruct((top, tok), BF),
            jax.ShapeDtypeStruct((width, ff), BF),
            jax.ShapeDtypeStruct((width, ff), BF),
            jax.ShapeDtypeStruct((ff, width), BF),
        ),
        in_specs=[vmem] * 4 + [hbm] * 3,
        out_specs=(vmem, vmem, hbm, hbm, hbm),
        scratch_shapes=[
            pltpu.VMEM((PEERS, 2, CAP, TILES, 128), BF),
            pltpu.VMEM((PEERS, 2, CAP, TILES, 128), BF),
            pltpu.VMEM((PEERS * CAP, width), BF),
            pltpu.VMEM((PEERS * CAP, width), BF),
            pltpu.VMEM((PEERS * CAP, ff), BF),
            pltpu.VMEM((PEERS * CAP, ff), BF),
            pltpu.VMEM((PEERS * CAP, ff), BF),
            pltpu.VMEM((width, ff), BF),
            pltpu.VMEM((width, ff), BF),
            pltpu.VMEM((ff, width), BF),
            pltpu.VMEM((PEERS * CAP, TILES, 128), BF),
            pltpu.VMEM((ROWS * TILES, 128), F32),
            pltpu.VMEM((PEERS, 1, 128), F32),
            pltpu.VMEM((PEERS, 1, 128), F32),
            pltpu.VMEM((tok, TILES, 128), BF),
            pltpu.VMEM((tok, TILES, 128), BF),
            pltpu.VMEM((PEERS, tok), F32),
            pltpu.VMEM((PEERS, 128), jnp.int32),
            pltpu.VMEM((PEERS, 128), F32),
            pltpu.VMEM((top, tok), jnp.int32),
            pltpu.SMEM((PEERS, 128), jnp.int32),
            pltpu.SMEM((PEERS, 128), F32),
            pltpu.SMEM((top, tok), jnp.int32),
            dma((3,)),
            dma((2,)),
            dma((3,)),
            dma((3,)),
            dma((GROUPS,)),
            dma((GROUPS,)),
            dma((GROUPS,)),
            dma((GROUPS,)),
            dma((GROUPS,)),
            dma((GROUPS,)),
        ],
        compiler_params=pltpu.CompilerParams(collective_id=0, has_side_effects=True, vmem_limit_bytes=60 << 20),
        cost_estimate=pl.CostEstimate(flops=29 * 10**9, bytes_accessed=20 * 10**6, transcendentals=10**6),
        name="routed_backward",
    )(
        expert_ids.T,
        gate_weights.T,
        tokens,
        out_grad,
        w_gate[0],
        w_up[0],
        w_down[0],
    )
    return (tg, gg.T, gwg[None], gwu[None], gwd[None])


def solution(mesh):
    both = ("gx", "gy")
    return jax.shard_map(
        on_device,
        mesh=mesh,
        in_specs=(P(both, None),) * 4 + (P(both, None, None),) * 3,
        out_specs=(P(both, None),) * 2 + (P(both, None, None),) * 3,
        check_vma=False,
    )
```

```python
import functools

import jax
import jax.numpy as jnp
from jax import lax
from jax.experimental import pallas as pl
from jax.experimental.pallas import tpu as pltpu
from jax.sharding import PartitionSpec as P

BF = jnp.bfloat16
F32 = jnp.float32
PEERS = 128
CAP = 9
GROUPS = 4
PARTS = 3
PART = CAP // PARTS
PER = PEERS // GROUPS
ROWS = PER * CAP
TILES = 16
MESH = pl.DeviceIdType.MESH
RIGHT = (((1,), (1,)), ((), ()))
CONTRACT = (((0,), (0,)), ((), ()))


def place(step, gx, gy, sign):
    i, j, k, c = lax.rem(step, 4), lax.rem(lax.div(step, 4), 4), lax.rem(lax.div(step, 16), 4), lax.div(step, 64)
    dx = 2 * i + 3 * j + k + 2 * c
    dy = 3 * i + c
    dz = 2 * i + 3 * k + 2 * c
    x, y, z, core = lax.div(gx, 4), lax.rem(gx, 4), lax.div(gy, 2), lax.rem(gy, 2)
    if sign < 0:
        dx, dy, dz = 32 - dx, 32 - dy, 32 - dz
    return lax.rem(x + dx, 4) * 4 + lax.rem(y + dy, 4), lax.rem(z + dz, 4) * 2 + lax.rem(core + c, 2)


def each(g, gx, gy, sign, act):
    x, y, z, core = lax.div(gx, 4), lax.rem(gx, 4), lax.div(gy, 2), lax.rem(gy, 2)
    c = g // 2
    other = lax.rem(core + c, 2)
    ys = [lax.rem(y + (3 * i + c if sign > 0 else 16 - 3 * i - c), 4) for i in range(4)]

    def serve(m, first):
        j, k = lax.rem(m, 4), lax.div(m, 4) + 2 * (g % 2)
        dx = 3 * j + k + 2 * c
        dz = 3 * k + 2 * c
        bx, bz = (x + dx, z + dz) if sign > 0 else (x + 32 - dx, z + 32 - dz)
        even = lax.rem(bx, 4) * 4, lax.rem(bz, 4) * 2 + other
        odd = lax.rem(bx + 2, 4) * 4, lax.rem(bz + 2, 4) * 2 + other
        for i in range(first, 4):
            a, b = odd if i % 2 else even
            act(g * PER + m * 4 + i, (a + ys[i], b))

    if g == 0:
        serve(jnp.int32(0), 1)

    def step(m, _):
        serve(m, 0)
        return 0

    lax.fori_loop(1 if g == 0 else 0, PER // 4, step, 0)


def kernel(
    ids, gates, tok, og, wg_h, wu_h, wd_h,
    tg, gg, gwg_h, gwu_h, gwd_h,
    sbuf, rbuf, x2, s2, act, gp, gu, wg, wu, wd, back, flat, gsend, gback,
    tokt, ogt, ranks, tok_v, gate_v, pair_v, slot_tok, slot_gate, pair_slot, table_sem,
    local_sem, w_sem, out_sem, ssem, rsem, bssem, brsem, gssem, grsem,
):
    gx, gy = lax.axis_index("gx"), lax.axis_index("gy")
    to = functools.partial(place, gx=gx, gy=gy)
    barrier = pltpu.get_barrier_semaphore()

    def greet(p, device):
        pl.semaphore_signal(barrier, inc=1, device_id=device, device_id_type=MESH)

    for g in range(GROUPS):
        each(g, gx, gy, 1, greet)
    loads = [pltpu.make_async_copy(h, v, w_sem.at[i]) for i, (h, v) in enumerate(((wg_h, wg), (wu_h, wu), (wd_h, wd)))]
    step_of = lax.broadcasted_iota(jnp.int32, (PEERS, 128), 0)
    tok_of = lax.broadcasted_iota(jnp.int32, (PEERS, 128), 1)
    ex, ey = to(step_of, sign=1)
    expert = ex * 8 + ey

    def named(k):
        return (expert == ids[k : k + 1, :]).astype(F32)

    gate_rows8 = gates[...].astype(F32)
    member = jnp.zeros((PEERS, 128), F32)
    gate_of = jnp.zeros((PEERS, 128), F32)
    for k in range(8):
        member += named(k)
        gate_of += named(k) * gate_rows8[k : k + 1, :]
    earlier = (step_of < tok_of).astype(F32).astype(BF)
    rank = jnp.dot(member.astype(BF), earlier, preferred_element_type=F32)
    ranks[...] = rank
    toks = jnp.zeros((PEERS, 128), F32)
    slot_gates = jnp.zeros((PEERS, 128), F32)
    tok_f = tok_of.astype(F32)
    for s in range(CAP):
        pick = jnp.where(rank == s, member, 0.0)
        toks = jnp.where(tok_of == s, jnp.sum(pick * tok_f, axis=1, keepdims=True), toks)
        slot_gates = jnp.where(tok_of == s, jnp.sum(pick * gate_of, axis=1, keepdims=True), slot_gates)
    tok_v[...] = jnp.clip(toks.astype(jnp.int32), 0, 127)
    gate_v[...] = slot_gates
    slots = step_of.astype(F32) * CAP + rank
    for k in range(8):
        slot = jnp.sum(named(k) * slots, axis=0, keepdims=True).astype(jnp.int32)
        pair_v[k : k + 1, :] = jnp.clip(slot, 0, PEERS * CAP - 1)
    tables = [
        pltpu.make_async_copy(v, m, table_sem.at[i])
        for i, (v, m) in enumerate(((tok_v, slot_tok), (gate_v, slot_gate), (pair_v, pair_slot)))
    ]
    for table in tables:
        table.start()
    def to_tiles(src, dst):
        for j in range(TILES):
            flat[pl.ds(j, 128, stride=TILES), :] = src[:, j * 128 : (j + 1) * 128].astype(F32)

        def tile(c, _):
            part = flat[pl.ds(pl.multiple_of(c * 8 * TILES, 8 * TILES), 8 * TILES), :]
            dst[pl.ds(pl.multiple_of(c * 8, 8), 8)] = part.astype(BF).reshape(8, TILES, 128)
            return 0

        lax.fori_loop(0, 16, tile, 0)

    to_tiles(tok, tokt)
    tables[0].wait()

    def gather_x(p, _):
        for s in range(CAP):
            sbuf[p, 0, s] = tokt[slot_tok[p, s]]
        return 0

    def gather_dy(p, _):
        for s in range(CAP):
            sbuf[p, 1, s] = (ogt[slot_tok[p, s]].astype(F32) * slot_gate[p, s]).astype(BF)
        return 0

    def send(p, device, half, g, part):
        rows = pl.ds(part * PART, PART)
        pltpu.make_async_remote_copy(
            sbuf.at[p, half, rows], rbuf.at[p, half, rows], ssem.at[g], rsem.at[g],
            device_id=device, device_id_type=MESH,
        ).start()

    for g in range(GROUPS):
        lo, hi = g * PER, (g + 1) * PER
        lax.fori_loop(lo, hi, gather_x, 0)
        if g == 0:
            pl.semaphore_wait(barrier, PEERS - 1)
        for part in range(PARTS):
            each(g, gx, gy, 1, functools.partial(send, half=0, g=g, part=part))
        if g == 0:
            to_tiles(og, ogt)
            tables[1].wait()
            tables[2].wait()
            for load in loads:
                load.start()
        lax.fori_loop(lo, hi, gather_dy, 0)
        for part in range(PARTS):
            each(g, gx, gy, 1, functools.partial(send, half=1, g=g, part=part))
    own = pltpu.make_async_copy(sbuf.at[0], rbuf.at[0], local_sem.at[0])
    own.start()
    for load in loads:
        load.wait()
    own.wait()

    def span(buf, g):
        return buf.at[pl.ds(1, PER - 1)] if g == 0 else buf.at[pl.ds(g * PER, PER)]

    def rows_span(buf, g):
        return buf.at[pl.ds(CAP, ROWS - CAP)] if g == 0 else buf.at[pl.ds(g * ROWS, ROWS)]

    def whole(src, dst, a, b):
        return pltpu.make_async_remote_copy(src, dst, a, b, device_id=to(1, sign=1), device_id_type=MESH)

    lane = lax.broadcasted_iota(jnp.int32, (ROWS, 128), 1)
    row = lax.broadcasted_iota(jnp.int32, (ROWS, 128), 0)
    own_lane = lane == row % CAP
    sel = lax.broadcasted_iota(jnp.int32, (PER, ROWS), 0) == lax.broadcasted_iota(jnp.int32, (PER, ROWS), 1) // CAP
    sel = sel.astype(F32).astype(BF)

    for g in range(GROUPS):
        whole(span(sbuf, g), span(rbuf, g), ssem.at[g], rsem.at[g]).wait()
        here = pl.ds(g * ROWS, ROWS)
        for half, dst in ((0, x2), (1, s2)):

            def spread(c, _, half=half):
                part = rbuf[g * PER + c, half].reshape(CAP * TILES, 128).astype(F32)
                flat[pl.ds(pl.multiple_of(c * CAP * TILES, CAP * TILES), CAP * TILES), :] = part
                return 0

            lax.fori_loop(0, PER, spread, 0)
            for j in range(TILES):
                dst[here, j * 128 : (j + 1) * 128] = flat[pl.ds(j, ROWS, stride=TILES), :].astype(BF)

        def hidden(c, total):
            cols = pl.ds(pl.multiple_of(c * 256, 256), 256)
            pre_gate = jnp.dot(x2[here, :], wg[:, cols], preferred_element_type=F32)
            pre_up = jnp.dot(x2[here, :], wu[:, cols], preferred_element_type=F32)
            sback = lax.dot_general(s2[here, :], wd[cols, :], RIGHT, preferred_element_type=F32)
            sigma = jax.nn.sigmoid(pre_gate)
            silu = pre_gate * sigma
            a = (silu * pre_up).astype(BF)
            act[here, cols] = a
            gu[here, cols] = (sback * silu).astype(BF)
            gp[here, cols] = (sback * pre_up * sigma * (1.0 + pre_gate * (1.0 - sigma))).astype(BF)
            return total + jnp.sum(sback * a.astype(F32), axis=1, keepdims=True)

        total = lax.fori_loop(0, 3, hidden, jnp.zeros((ROWS, 1), F32))
        spread_gate = jnp.where(own_lane, total, 0.0).astype(BF)
        gate_rows = jnp.dot(sel, spread_gate, preferred_element_type=F32)
        for c in range(PER):
            gsend[g * PER + c] = gate_rows[c : c + 1, :]

        def inputs(n, _):
            rows = pl.ds(pl.multiple_of(n * 256, 256), 256)
            part = lax.dot_general(gp[here, :], wg[rows, :], RIGHT, preferred_element_type=F32)
            part += lax.dot_general(gu[here, :], wu[rows, :], RIGHT, preferred_element_type=F32)
            flat[pl.ds(2 * n, ROWS, stride=TILES), :] = part[:, :128]
            flat[pl.ds(2 * n + 1, ROWS, stride=TILES), :] = part[:, 128:]
            return 0

        lax.fori_loop(0, 8, inputs, 0)

        def pack(c, _):
            part = flat[pl.ds(pl.multiple_of(c * CAP * TILES, CAP * TILES), CAP * TILES), :]
            sbuf[g * PER + c, 0] = part.astype(BF).reshape(CAP, TILES, 128)
            return 0

        lax.fori_loop(0, PER, pack, 0)

        def give(p, device, part):
            pltpu.make_async_remote_copy(
                sbuf.at[p, 0, pl.ds(part * PART, PART)], back.at[pl.ds(p * CAP + part * PART, PART)],
                bssem.at[g], brsem.at[g], device_id=device, device_id_type=MESH,
            ).start()

        def give_gate(p, device):
            pltpu.make_async_remote_copy(
                gsend.at[p], gback.at[p], gssem.at[g], grsem.at[g], device_id=device, device_id_type=MESH
            ).start()

        if g == 0:
            own_back = pltpu.make_async_copy(sbuf.at[0, 0], back.at[pl.ds(0, CAP)], local_sem.at[0])
            own_gate = pltpu.make_async_copy(gsend.at[0], gback.at[0], local_sem.at[1])
            own_back.start()
            own_gate.start()
        each(g, gx, gy, -1, give_gate)
        for part in range(PARTS):
            each(g, gx, gy, -1, functools.partial(give, part=part))

    def w_in(n, _):
        rows = pl.ds(pl.multiple_of(n * 256, 256), 256)
        xt = x2[:, rows]
        wg[rows, :] = lax.dot_general(xt, gp[...], CONTRACT, preferred_element_type=F32).astype(BF)
        wu[rows, :] = lax.dot_general(xt, gu[...], CONTRACT, preferred_element_type=F32).astype(BF)
        return 0

    def w_out(n, _):
        rows = pl.ds(pl.multiple_of((n // 2) * 256, 256), 256)
        cols = pl.ds(pl.multiple_of((n % 2) * 1024, 1024), 1024)
        wd[rows, cols] = lax.dot_general(act[:, rows], s2[:, cols], CONTRACT, preferred_element_type=F32).astype(BF)
        return 0

    stores = [pltpu.make_async_copy(v, h, out_sem.at[i]) for i, (h, v) in enumerate(((gwg_h, wg), (gwu_h, wu), (gwd_h, wd)))]
    lax.fori_loop(0, 8, w_in, 0)
    stores[0].start()
    stores[1].start()
    lax.fori_loop(0, 6, w_out, 0)
    stores[2].start()

    own_back.wait()
    own_gate.wait()
    for g in range(GROUPS):
        whole(span(gsend, g), span(gback, g), gssem.at[g], grsem.at[g]).wait()
    table = gback[...].reshape(PEERS, 128)
    rank = ranks[...]
    found = jnp.zeros((PEERS, 128), F32)
    for s in range(CAP):
        found = jnp.where(rank == s, table[:, s : s + 1], found)
    ex, ey = to(step_of, sign=1)
    expert = ex * 8 + ey
    for k in range(8):
        value = jnp.sum((expert == ids[k : k + 1, :]).astype(F32) * found, axis=0, keepdims=True)
        gg[k : k + 1, :] = (value / gates[k : k + 1, :].astype(F32)).astype(BF)
    for g in range(GROUPS):
        first = 1 if g == 0 else 0
        src = sbuf.at[pl.ds(g * PER + first, PER - first), 0]
        whole(src, rows_span(back, g), bssem.at[g], brsem.at[g]).wait()

    def combine(t, _):
        total = back[pair_slot[0, t]].astype(F32)
        for k in range(1, 8):
            total += back[pair_slot[k, t]].astype(F32)
        flat[pl.ds(pl.multiple_of(t * TILES, TILES), TILES), :] = total
        return 0

    lax.fori_loop(0, 128, combine, 0)
    for j in range(TILES):
        tg[:, j * 128 : (j + 1) * 128] = flat[pl.ds(j, 128, stride=TILES), :].astype(BF)
    for store in stores:
        store.wait()


def on_device(tokens, out_grad, expert_ids, gate_weights, w_gate, w_up, w_down):
    tok, top = expert_ids.shape
    width, ff = w_gate.shape[1:]
    vmem, hbm = pl.BlockSpec(memory_space=pltpu.VMEM), pl.BlockSpec(memory_space=pl.ANY)
    dma = pltpu.SemaphoreType.DMA
    tg, gg, gwg, gwu, gwd = pl.pallas_call(
        kernel,
        out_shape=(
            jax.ShapeDtypeStruct((tok, width), BF),
            jax.ShapeDtypeStruct((top, tok), BF),
            jax.ShapeDtypeStruct((width, ff), BF),
            jax.ShapeDtypeStruct((width, ff), BF),
            jax.ShapeDtypeStruct((ff, width), BF),
        ),
        in_specs=[vmem] * 4 + [hbm] * 3,
        out_specs=(vmem, vmem, hbm, hbm, hbm),
        scratch_shapes=[
            pltpu.VMEM((PEERS, 2, CAP, TILES, 128), BF),
            pltpu.VMEM((PEERS, 2, CAP, TILES, 128), BF),
            pltpu.VMEM((PEERS * CAP, width), BF),
            pltpu.VMEM((PEERS * CAP, width), BF),
            pltpu.VMEM((PEERS * CAP, ff), BF),
            pltpu.VMEM((PEERS * CAP, ff), BF),
            pltpu.VMEM((PEERS * CAP, ff), BF),
            pltpu.VMEM((width, ff), BF),
            pltpu.VMEM((width, ff), BF),
            pltpu.VMEM((ff, width), BF),
            pltpu.VMEM((PEERS * CAP, TILES, 128), BF),
            pltpu.VMEM((ROWS * TILES, 128), F32),
            pltpu.VMEM((PEERS, 1, 128), F32),
            pltpu.VMEM((PEERS, 1, 128), F32),
            pltpu.VMEM((tok, TILES, 128), BF),
            pltpu.VMEM((tok, TILES, 128), BF),
            pltpu.VMEM((PEERS, tok), F32),
            pltpu.VMEM((PEERS, 128), jnp.int32),
            pltpu.VMEM((PEERS, 128), F32),
            pltpu.VMEM((top, tok), jnp.int32),
            pltpu.SMEM((PEERS, 128), jnp.int32),
            pltpu.SMEM((PEERS, 128), F32),
            pltpu.SMEM((top, tok), jnp.int32),
            dma((3,)),
            dma((2,)),
            dma((3,)),
            dma((3,)),
            dma((GROUPS,)),
            dma((GROUPS,)),
            dma((GROUPS,)),
            dma((GROUPS,)),
            dma((GROUPS,)),
            dma((GROUPS,)),
        ],
        compiler_params=pltpu.CompilerParams(collective_id=0, has_side_effects=True, vmem_limit_bytes=60 << 20),
        cost_estimate=pl.CostEstimate(flops=29 * 10**9, bytes_accessed=20 * 10**6, transcendentals=10**6),
        name="routed_backward",
    )(
        expert_ids.T,
        gate_weights.T,
        tokens,
        out_grad,
        w_gate[0],
        w_up[0],
        w_down[0],
    )
    return (tg, gg.T, gwg[None], gwu[None], gwd[None])


def solution(mesh):
    both = ("gx", "gy")
    return jax.shard_map(
        on_device,
        mesh=mesh,
        in_specs=(P(both, None),) * 4 + (P(both, None, None),) * 3,
        out_specs=(P(both, None),) * 2 + (P(both, None, None),) * 3,
        check_vma=False,
    )
```
